32 devices in a mesh: dom: 2 (over y), bank: 2 (over core), grp: 8 (over z, x).
Axes of the slice: x: 2, y: 2, z: 4, core: 2. Of those that a mesh axis runs over, the one named last changes fastest.
Arguments:
- embeddings: bfloat16 [8192, 768], P(('dom', 'bank', 'grp')), parts along dimension 0
- cluster_of: int32 [8192], P(('dom', 'bank', 'grp')), parts along dimension 0, may hold values from 0 to 3, as said below
- dest_list: int32 [32, 16, 32], P(('dom', 'bank', 'grp')), parts along dimension 0, may hold values from -1 to 255, as said below
Outputs:
- best_sim: float32 [8192], P(('dom', 'bank', 'grp')), parts along dimension 0
The draws below stay inside these ranges and needn't reach their ends.
There are 2 independent parts, one for each index of `dom`. The reference program is written for one: setup_inputs(seed, part) draws one part's arguments, and reference() takes and returns one part's arrays. A program takes and returns all parts, laid end to end along the dimension named above; each array names one. Nothing has to cross between parts.
Inputs may be any that keep to these rules, and one draw needn't show every extreme that they name: For each crawl shard s, each of its 256 local rows appears exactly once in dest_list[s]; in each list dest_list[s, d] the used slots come first and the rest hold -1; every destination device receives exactly 256 rows in all; in every draw some shard fills all 32 slots to some destination. A row's cluster lies in slab (cluster_of // 2), which equals the bank index of the device that dest_list sends the row to.
All inputs are finite; a program needn't handle non-finite values.
Results may differ from the reference program's by a relative error of at most 0.0025.
Values may be sent and summed in bfloat16 or wider, within the bound.
A program may use at most 128 MiB of HBM per device.

```python
import math
import jax
import jax.numpy as jnp
from jax import lax

D = 768
ROWS_DEV = 256
CLUSTERS_SLAB = 2
CAP = 32
CLUSTERS = 4
ROWS = 4096
N_BANK = 2
N_GRP = 8


def routing(key):
    key = jax.random.fold_in(key, 101)
    count_dev = N_BANK * N_GRP
    half_count = count_dev // 2
    cap_half = CAP // 2
    first_key, second_key, third_key = jax.random.split(key, 3)
    lifted = jax.random.randint(first_key, (half_count,), 0, cap_half + 1).at[0].set(cap_half)
    loads = jnp.concatenate([cap_half + lifted, cap_half - lifted]).astype(jnp.int32)
    offset = jax.random.randint(second_key, (), 0, count_dev)
    source = jnp.arange(count_dev, dtype=jnp.int32)[:, None]
    target = jnp.arange(count_dev, dtype=jnp.int32)[None, :]
    counts = loads[(target - source + offset) % count_dev]
    starts = jnp.cumsum(counts, axis=1) - counts
    orders = jax.vmap(lambda sub_key: jax.random.permutation(sub_key, ROWS_DEV))(jax.random.split(third_key, count_dev)).astype(jnp.int32)
    slot_index = jnp.arange(CAP, dtype=jnp.int32)
    picks = jnp.clip(starts[:, :, None] + slot_index, 0, ROWS_DEV - 1).reshape(count_dev, -1)
    rows = jnp.take_along_axis(orders, picks, axis=1).reshape(count_dev, count_dev, CAP)
    is_live = slot_index[None, None, :] < counts[:, :, None]
    return (jnp.where(is_live, rows, -1).astype(jnp.int32), is_live)


def assign(key):
    slot_rows, is_live = routing(key)
    key = jax.random.fold_in(key, 202)
    count_dev = N_BANK * N_GRP
    source = jnp.arange(count_dev, dtype=jnp.int32)[:, None, None]
    target = jnp.arange(count_dev, dtype=jnp.int32)[None, :, None]
    crawl_row = jnp.where(is_live, source * ROWS_DEV + slot_rows, ROWS)
    slab_value = jnp.broadcast_to(target // N_GRP, slot_rows.shape).astype(jnp.int32)
    slab_row = jnp.zeros((ROWS,), jnp.int32).at[crawl_row.reshape(-1)].set(slab_value.reshape(-1), mode='drop')
    return slab_row * CLUSTERS_SLAB + jax.random.randint(key, (ROWS,), 0, CLUSTERS_SLAB).astype(jnp.int32)


def draw_dest_list(key, part):
    return routing(key)[0]


def draw_cluster_of(key, part):
    return assign(key)


def draw_embeddings(key, part):
    clusters = assign(key)
    key = jax.random.fold_in(key, 3)
    center_key = jax.random.fold_in(key, 0)
    strength_key = jax.random.fold_in(key, 1)
    noise_key = jax.random.fold_in(key, 2)
    common_key = jax.random.fold_in(key, 4)
    pick_key = jax.random.fold_in(key, 5)
    jitter_key = jax.random.fold_in(key, 6)
    common = jax.random.normal(common_key, (1, D), jnp.float32)
    centers = 2.0 * common + jax.random.normal(center_key, (CLUSTERS, D), jnp.float32)
    strength = jnp.exp(jax.random.uniform(strength_key, (ROWS, 1), jnp.float32, math.log(0.3), math.log(3.0)))
    noise = jax.random.normal(noise_key, (ROWS, D), jnp.float32)
    base = strength * centers[clusters] + noise
    eligible_key, copy_key, which_key = jax.random.split(pick_key, 3)
    eligible = jax.random.randint(eligible_key, (ROWS,), 0, 2).astype(jnp.int32)
    inclusive = jnp.cumsum(eligible).astype(jnp.int32)
    before = inclusive - eligible
    wants = jax.random.randint(copy_key, (ROWS,), 0, 8).astype(jnp.int32)
    is_copy = (eligible == 0) & (wants == 0) & (before >= 1)
    picked = jax.random.randint(which_key, (ROWS,), 0, jnp.maximum(before, 1)).astype(jnp.int32)
    source = jnp.clip(jnp.searchsorted(inclusive, picked, side='right').astype(jnp.int32), 0, ROWS - 1)
    jitter = 0.05 * jax.random.normal(jitter_key, (ROWS, D), jnp.float32)
    rows = jnp.where(is_copy[:, None], base[source] + jitter, base)
    return rows.astype(jnp.bfloat16)


def setup_inputs(seed: int = 0, part: int = 0) -> dict:
    arg_keys = jax.random.split(jax.random.key(seed), 4)
    part_keys = jax.random.split(jax.random.fold_in(arg_keys[3], part), 4)
    return {
        "embeddings": draw_embeddings(jax.random.fold_in(jax.random.fold_in(arg_keys[3], part), 71), part),
        "cluster_of": draw_cluster_of(jax.random.fold_in(jax.random.fold_in(arg_keys[3], part), 71), part),
        "dest_list": draw_dest_list(jax.random.fold_in(jax.random.fold_in(arg_keys[3], part), 71), part),
    }


small_eps = 1e-06

def reference(embeddings, cluster_of, dest_list):
    count_dev = dest_list.shape[0]
    total = embeddings.shape[0]
    rows_dev = total // count_dev
    widened = embeddings.astype(jnp.float32)
    unit_rows = (widened * lax.rsqrt(lax.optimization_barrier(jnp.sum(widened * widened, axis=1, keepdims=True)) + small_eps)).astype(jnp.bfloat16)
    source = jnp.arange(count_dev, dtype=jnp.int32)[:, None, None]
    target_dev = jnp.arange(count_dev, dtype=jnp.int32)[None, :, None]
    crawl_row = jnp.where(dest_list >= 0, source * rows_dev + dest_list, total).astype(jnp.int32)
    slab_value = jnp.broadcast_to(target_dev // N_GRP, dest_list.shape).astype(jnp.int32)
    slab_of = jnp.full((total,), -1, jnp.int32).at[crawl_row.reshape(-1)].set(slab_value.reshape(-1), mode='drop')
    present = slab_of >= 0
    block_rows = math.gcd(total, 1024)
    wide_rows = unit_rows.astype(jnp.float32)
    order = jnp.arange(total, dtype=jnp.int32)

    def one_block(first_row):
        first_row = first_row.astype(jnp.int32)
        query = lax.dynamic_slice_in_dim(wide_rows, first_row, block_rows, 0)
        query_cluster = lax.dynamic_slice_in_dim(cluster_of, first_row, block_rows, 0)
        query_slab = lax.dynamic_slice_in_dim(slab_of, first_row, block_rows, 0)
        query_order = lax.dynamic_slice_in_dim(order, first_row, block_rows, 0)
        scores = jnp.dot(query, wide_rows.T, precision=lax.Precision.HIGHEST)
        allowed = (query_cluster[:, None] == cluster_of[None, :]) & (query_slab[:, None] == slab_of[None, :])
        allowed = allowed & present[None, :] & (order[None, :] < query_order[:, None])
        return lax.optimization_barrier(jnp.max(jnp.where(allowed, scores, -1.0), axis=1))
    starts = jnp.arange(0, total, block_rows, dtype=jnp.int32)
    best_sim = lax.map(one_block, starts).reshape(-1)
    return jnp.where(present, best_sim, -1.0).astype(jnp.float32)
```

```python
import functools
import jax
import jax.numpy as jnp
from jax import lax
from jax.experimental import pallas as pl
from jax.experimental.pallas import tpu as pltpu
from jax.sharding import PartitionSpec as P

small_eps = 1e-06
MESH = pl.DeviceIdType.MESH


def masked_scores(query_rows, query_cluster, other_rows, other_cluster):
    scores = lax.dot_general(
        query_rows, other_rows, (((1,), (1,)), ((), ())), preferred_element_type=jnp.float32
    )
    matching = query_cluster[:, None] == other_cluster[None, :]
    return (scores, matching)


def routed_on_device(embeddings, cluster_of, dest_list):
    rows_dev = embeddings.shape[0]
    width = embeddings.shape[1]
    devices_part = dest_list.shape[1]
    capacity = dest_list.shape[2]
    source = lax.axis_index(("bank", "grp"))
    widened = embeddings.astype(jnp.float32)
    unit_rows = (
        widened * lax.rsqrt(jnp.sum(widened * widened, axis=1, keepdims=True) + small_eps)
    ).astype(jnp.bfloat16)
    slot_rows = dest_list[0]
    is_live = slot_rows >= 0
    safe_rows = jnp.where(is_live, slot_rows, 0)
    outgoing = jnp.take(unit_rows, safe_rows.reshape(-1), axis=0).reshape(
        devices_part, capacity, width
    )
    out_cluster = jnp.where(is_live, jnp.take(cluster_of, safe_rows), -1)
    out_crawl = jnp.where(is_live, source * rows_dev + safe_rows, -1)
    arrived, in_cluster, in_crawl = (
        lax.all_to_all(outgoing, ("bank", "grp"), split_axis=0, concat_axis=0, tiled=True),
        lax.all_to_all(out_cluster, ("bank", "grp"), split_axis=0, concat_axis=0, tiled=True),
        lax.all_to_all(out_crawl, ("bank", "grp"), split_axis=0, concat_axis=0, tiled=True),
    )
    flat_cluster = in_cluster.reshape(-1)
    flat_crawl = in_crawl.reshape(-1)
    present = flat_cluster >= 0
    position = jnp.cumsum(present.astype(jnp.int32)) - 1
    chosen = (position[None, :] == jnp.arange(rows_dev, dtype=jnp.int32)[:, None]) & present[
        None, :
    ]
    key_rows = jnp.dot(
        chosen.astype(jnp.bfloat16), arrived.reshape(-1, width), preferred_element_type=jnp.float32
    ).astype(jnp.bfloat16)
    key_cluster = jnp.sum(jnp.where(chosen, flat_cluster[None, :], 0), axis=1)
    key_crawl = jnp.sum(jnp.where(chosen, flat_crawl[None, :], 0), axis=1)
    floor_value = jnp.full((rows_dev,), -1.0, jnp.float32)
    scores, matching = masked_scores(
        key_rows,
        key_cluster,
        lax.all_gather(key_rows, "grp", axis=0, tiled=True),
        lax.all_gather(key_cluster, "grp", axis=0, tiled=True),
    )
    earlier = matching & (
        lax.all_gather(key_crawl, "grp", axis=0, tiled=True)[None, :] < key_crawl[:, None]
    )
    best_sim = jnp.maximum(floor_value, jnp.max(jnp.where(earlier, scores, -1.0), axis=1))
    slot_best = jnp.where(
        present, jnp.take(best_sim, jnp.clip(position, 0, rows_dev - 1)), -1.0
    ).reshape(devices_part, capacity)
    returned_best = lax.all_to_all(
        slot_best, ("bank", "grp"), split_axis=0, concat_axis=0, tiled=True
    )
    result = (
        jnp.full((rows_dev,), -1.0, jnp.float32)
        .at[safe_rows.reshape(-1)]
        .max(jnp.where(is_live, returned_best, -1.0).reshape(-1))
    )
    return result


LOW = 8


def pair_kernel(
    emb_ref, cluster_ref, dest_ref, out_ref,
    blocks, meta, columns, best, returned, own_meta,
    block_send, meta_send, block_recv, meta_recv, best_send, best_recv,
):
    rows = emb_ref.shape[0]
    n_dest = dest_ref.shape[0]
    bank = lax.axis_index("bank")
    grp = lax.axis_index("grp")
    z = grp // 2
    x = grp % 2
    high = z // 2
    inner_z = 1 + high
    is_inner = z == inner_z
    mine = 2 * x + bank
    outer_add = jnp.where(is_inner, 0, 4)
    own = mine + outer_add

    barrier = pltpu.get_barrier_semaphore()
    for b in range(2):
        for g in range(8):

            @pl.when((bank != b) | (grp != g))
            def _():
                pl.semaphore_signal(
                    barrier, inc=1, device_id={"bank": b, "grp": g}, device_id_type=MESH
                )

    wide = emb_ref[...].astype(jnp.float32)
    scale = lax.rsqrt(jnp.sum(wide * wide, axis=1, keepdims=True) + small_eps)
    blocks[own] = (wide * scale).astype(jnp.bfloat16)

    row_id = lax.broadcasted_iota(jnp.int32, (dest_ref.shape[1], rows), 1)
    dest_columns = jnp.transpose(dest_ref[...].astype(jnp.float32)).astype(jnp.int32)
    slab_wide = jnp.full(row_id.shape, -1, jnp.int32)
    for d in range(n_dest):
        named = dest_columns[:, d : d + 1] == row_id
        slab_wide = jnp.maximum(slab_wide, jnp.where(named, d // (n_dest // 2), -1))
    slab = jnp.max(slab_wide, axis=0, keepdims=True)
    key = jnp.where(slab >= 0, cluster_ref[...] * 2 + slab, -1).astype(jnp.float32)
    own_meta[...] = jnp.broadcast_to(key, own_meta.shape)
    meta[own] = jnp.broadcast_to(key, own_meta.shape)
    best[...] = jnp.full(best.shape, -1.0, jnp.float32)

    pl.semaphore_wait(barrier, 15)

    def send(index, slot, to_slot, to_bank, to_grp):
        device = {"bank": to_bank, "grp": to_grp}
        for buffer, sent, got in (
            (meta, meta_send, meta_recv), (blocks, block_send, block_recv)
        ):
            pltpu.make_async_remote_copy(
                src_ref=buffer.at[slot], dst_ref=buffer.at[to_slot],
                send_sem=sent.at[index], recv_sem=got.at[to_slot],
                device_id=device, device_id_type=MESH,
            ).start()

    def sent(index, slot):
        for buffer, sem, got in (
            (meta, meta_send, meta_recv), (blocks, block_send, block_recv)
        ):
            pltpu.make_async_remote_copy(
                src_ref=buffer.at[slot], dst_ref=buffer.at[slot],
                send_sem=sem.at[index], recv_sem=got.at[slot],
                device_id={"bank": 1 - bank, "grp": grp}, device_id_type=MESH,
            ).wait_send()

    def arrive(slot):
        for buffer, sem, got in (
            (meta, meta_send, meta_recv), (blocks, block_send, block_recv)
        ):
            pltpu.make_async_remote_copy(
                src_ref=buffer.at[slot], dst_ref=buffer.at[slot],
                send_sem=sem.at[0], recv_sem=got.at[slot],
                device_id={"bank": 1 - bank, "grp": grp}, device_id_type=MESH,
            ).wait_recv()

    def column(slot):
        wide_key = jnp.broadcast_to(meta[slot][:1], (128, rows))
        columns[slot] = jnp.transpose(wide_key)

    def slot_of(rel, outer):
        sx = (x + rel // 2) % 2
        sb = (bank + rel % 2) % 2
        slot = 2 * sx + sb + 4 * outer
        sz = inner_z if outer == 0 else 3 * high
        return slot, sb * 8 + sz * 2 + sx

    def scores_into(k_slot, q_slot, diagonal):
        s = lax.dot_general(
            blocks[k_slot], blocks[q_slot], (((1,), (1,)), ((), ())),
            preferred_element_type=jnp.float32,
        )
        k_key = columns[k_slot]
        q_key = meta[q_slot][:1]
        for h in range(rows // 128):
            part = slice(h * 128, (h + 1) * 128)
            allowed = k_key == q_key[:, part]
            if diagonal:
                k_id = lax.broadcasted_iota(jnp.int32, (rows, 128), 0)
                q_id = lax.broadcasted_iota(jnp.int32, (rows, 128), 1) + h * 128
                allowed = allowed & (k_id < q_id)
            kept = jnp.where(allowed, s[:, part], -1.0)
            top = jnp.max(kept.reshape(rows // 8, 8, 128), axis=0)
            best[q_slot, :, part] = jnp.maximum(best[q_slot, :, part], top)

    def earlier(k, q):
        @pl.when(k[1] < q[1])
        def _():
            scores_into(k[0], q[0], False)

    def low_pair(which, rel, outer):
        slot, shard = slot_of(rel, outer)
        swap = bank * (1 - (bank + rel % 2) % 2)
        k_slot = (LOW + which) * (1 - swap) + slot * swap
        q_slot = (LOW + which) * swap + slot * (1 - swap)
        scores_into(k_slot, q_slot, False)

    @pl.when(jnp.logical_not(is_inner))
    def _():
        send(0, own, own, bank, inner_z * 2 + x)

    @pl.when(is_inner)
    def _():
        x_grp = z * 2 + (1 - x)
        in0, in1, in2, in3 = (slot_of(r, 0) for r in range(4))
        out0, out1, out2, out3 = (slot_of(r, 1) for r in range(4))

        @pl.when(z == 1)
        def _():
            send(0, own, LOW, bank, grp + 2)

        send(1, own, own, bank, x_grp)
        send(2, own, own, 1 - bank, grp)
        column(in0[0])
        scores_into(in0[0], in0[0], True)
        arrive(in1[0])
        column(in1[0])
        earlier(in1, in0)

        arrive(out0[0])

        @pl.when(z == 1)
        def _():
            send(3, out0[0], LOW + 1, bank, grp + 2)

        send(4, out0[0], out0[0], bank, x_grp)
        send(5, out0[0], out0[0], 1 - bank, grp)
        arrive(in2[0])
        send(6, in2[0], in2[0], 1 - bank, grp)
        column(out0[0])
        column(in2[0])
        scores_into(out0[0], out0[0], True)
        for k, q in ((out0, in0), (in0, out0), (in1, out0), (in2, in0), (in2, out0)):
            earlier(k, q)
        for k in (out1, in3):
            arrive(k[0])
            column(k[0])
            earlier(k, in0)
            earlier(k, out0)

        @pl.when(z == 2)
        def _():
            arrive(LOW)
            column(LOW)

            @pl.loop(0, 4)
            def _(rel):
                low_pair(0, rel, 0)

            @pl.loop(0, 2)
            def _(rel):
                low_pair(0, rel, 1)

        arrive(out2[0])
        send(7, out2[0], out2[0], 1 - bank, grp)
        for k in (out2, out3):
            if k is out3:
                arrive(k[0])
            column(k[0])
            earlier(k, in0)
            earlier(k, out0)

        @pl.when(z == 2)
        def _():
            @pl.loop(2, 4)
            def _(rel):
                low_pair(0, rel, 1)

            arrive(LOW + 1)
            column(LOW + 1)

            @pl.loop(0, 4)
            def _(rel):
                low_pair(1, rel, 0)

            @pl.loop(0, 4)
            def _(rel):
                low_pair(1, rel, 1)

    def best_copy(index, slot, to, to_bank, to_grp):
        return pltpu.make_async_remote_copy(
            src_ref=best.at[slot], dst_ref=returned.at[to],
            send_sem=best_send.at[index], recv_sem=best_recv.at[to],
            device_id={"bank": to_bank, "grp": to_grp}, device_id_type=MESH,
        )

    @pl.when(z == 1)
    def _():
        best_copy(0, mine + 4, 0, bank, grp - 2).start()

    @pl.when(z == 2)
    def _():
        for rel in range(4):
            slot, _ = slot_of(rel, 0)
            to_bank = (bank + rel % 2) % 2
            to_x = (x + rel // 2) % 2
            best_copy(rel, slot + 4, mine, to_bank, 6 + to_x).start()
            if rel:
                best_copy(4 + rel, slot, mine, to_bank, 4 + to_x).start()

        @pl.when(bank == 1)
        def _():
            best_copy(4, LOW, 1, bank, grp - 2).start()
            best_copy(8, LOW + 1, 1, bank, grp - 4).start()

    def take(index):
        best_copy(0, own, index, 1 - bank, grp).wait_recv()
        best[own] = jnp.maximum(best[own], returned[index])

    def best_sent(index):
        best_copy(index, own, 0, 1 - bank, grp).wait_send()

    @pl.when(z == 0)
    def _():
        take(0)

    @pl.when((z < 2) & (bank == 1))
    def _():
        take(1)

    @pl.when(z >= 2)
    def _():
        for index in range(4):

            @pl.when((z == 3) | (mine != index))
            def _():
                take(index)

    top = jnp.max(best[own], axis=0, keepdims=True)
    out_ref[...] = jnp.where(own_meta[:1] >= 0, top, -1.0)

    @pl.when(jnp.logical_not(is_inner))
    def _():
        sent(0, own)

    @pl.when(is_inner)
    def _():
        for index in (1, 2, 4, 5, 6, 7):
            sent(index, own)

    @pl.when(z == 1)
    def _():
        sent(0, own)
        sent(3, own)
        best_sent(0)

    @pl.when(z == 2)
    def _():
        for index in (0, 1, 2, 3, 5, 6, 7):
            best_sent(index)

        @pl.when(bank == 1)
        def _():
            best_sent(4)
            best_sent(8)


def paired_on_device(embeddings, cluster_of, dest_list):
    rows, width = embeddings.shape
    dma = pltpu.SemaphoreType.DMA
    vmem = pl.BlockSpec(memory_space=pltpu.VMEM)
    result = pl.pallas_call(
        pair_kernel,
        out_shape=jax.ShapeDtypeStruct((1, rows), jnp.float32),
        in_specs=[vmem] * 3,
        out_specs=vmem,
        scratch_shapes=[
            pltpu.VMEM((10, rows, width), jnp.bfloat16),
            pltpu.VMEM((10, 8, rows), jnp.float32),
            pltpu.VMEM((10, rows, 128), jnp.float32),
            pltpu.VMEM((10, 8, rows), jnp.float32),
            pltpu.VMEM((4, 8, rows), jnp.float32),
            pltpu.VMEM((8, rows), jnp.float32),
            dma((8,)), dma((8,)), dma((10,)), dma((10,)), dma((9,)), dma((4,)),
        ],
        compiler_params=pltpu.CompilerParams(
            collective_id=0, has_side_effects=True, vmem_limit_bytes=40 * 2**20
        ),
        cost_estimate=pl.CostEstimate(
            flops=16 * 2 * rows * rows * width, bytes_accessed=rows * width * 2, transcendentals=rows
        ),
    )(embeddings, cluster_of.reshape(1, rows), dest_list[0])
    return result.reshape(rows)


def solution(mesh):
    paired = mesh.shape["bank"] == 2 and mesh.shape["grp"] == 8
    return jax.shard_map(
        paired_on_device if paired else routed_on_device,
        mesh=mesh,
        in_specs=(
            P(("dom", "bank", "grp"), None),
            P(("dom", "bank", "grp")),
            P(("dom", "bank", "grp"), None, None),
        ),
        out_specs=P(("dom", "bank", "grp")),
        check_vma=False,
    )
```

```python
import functools
import jax
import jax.numpy as jnp
from jax import lax
from jax.experimental import pallas as pl
from jax.experimental.pallas import tpu as pltpu
from jax.sharding import PartitionSpec as P

small_eps = 1e-06
MESH = pl.DeviceIdType.MESH


def masked_scores(query_rows, query_cluster, other_rows, other_cluster):
    scores = lax.dot_general(
        query_rows, other_rows, (((1,), (1,)), ((), ())), preferred_element_type=jnp.float32
    )
    matching = query_cluster[:, None] == other_cluster[None, :]
    return (scores, matching)


def routed_on_device(embeddings, cluster_of, dest_list):
    rows_dev = embeddings.shape[0]
    width = embeddings.shape[1]
    devices_part = dest_list.shape[1]
    capacity = dest_list.shape[2]
    source = lax.axis_index(("bank", "grp"))
    widened = embeddings.astype(jnp.float32)
    unit_rows = (
        widened * lax.rsqrt(jnp.sum(widened * widened, axis=1, keepdims=True) + small_eps)
    ).astype(jnp.bfloat16)
    slot_rows = dest_list[0]
    is_live = slot_rows >= 0
    safe_rows = jnp.where(is_live, slot_rows, 0)
    outgoing = jnp.take(unit_rows, safe_rows.reshape(-1), axis=0).reshape(
        devices_part, capacity, width
    )
    out_cluster = jnp.where(is_live, jnp.take(cluster_of, safe_rows), -1)
    out_crawl = jnp.where(is_live, source * rows_dev + safe_rows, -1)
    arrived, in_cluster, in_crawl = (
        lax.all_to_all(outgoing, ("bank", "grp"), split_axis=0, concat_axis=0, tiled=True),
        lax.all_to_all(out_cluster, ("bank", "grp"), split_axis=0, concat_axis=0, tiled=True),
        lax.all_to_all(out_crawl, ("bank", "grp"), split_axis=0, concat_axis=0, tiled=True),
    )
    flat_cluster = in_cluster.reshape(-1)
    flat_crawl = in_crawl.reshape(-1)
    present = flat_cluster >= 0
    position = jnp.cumsum(present.astype(jnp.int32)) - 1
    chosen = (position[None, :] == jnp.arange(rows_dev, dtype=jnp.int32)[:, None]) & present[
        None, :
    ]
    key_rows = jnp.dot(
        chosen.astype(jnp.bfloat16), arrived.reshape(-1, width), preferred_element_type=jnp.float32
    ).astype(jnp.bfloat16)
    key_cluster = jnp.sum(jnp.where(chosen, flat_cluster[None, :], 0), axis=1)
    key_crawl = jnp.sum(jnp.where(chosen, flat_crawl[None, :], 0), axis=1)
    floor_value = jnp.full((rows_dev,), -1.0, jnp.float32)
    scores, matching = masked_scores(
        key_rows,
        key_cluster,
        lax.all_gather(key_rows, "grp", axis=0, tiled=True),
        lax.all_gather(key_cluster, "grp", axis=0, tiled=True),
    )
    earlier = matching & (
        lax.all_gather(key_crawl, "grp", axis=0, tiled=True)[None, :] < key_crawl[:, None]
    )
    best_sim = jnp.maximum(floor_value, jnp.max(jnp.where(earlier, scores, -1.0), axis=1))
    slot_best = jnp.where(
        present, jnp.take(best_sim, jnp.clip(position, 0, rows_dev - 1)), -1.0
    ).reshape(devices_part, capacity)
    returned_best = lax.all_to_all(
        slot_best, ("bank", "grp"), split_axis=0, concat_axis=0, tiled=True
    )
    result = (
        jnp.full((rows_dev,), -1.0, jnp.float32)
        .at[safe_rows.reshape(-1)]
        .max(jnp.where(is_live, returned_best, -1.0).reshape(-1))
    )
    return result


LOW = 8


def pair_kernel(
    emb_hbm, cluster_hbm, dest_hbm, out_ref,
    emb_ref, cluster_ref, dest_ref, blocks, meta, columns, best, returned, own_meta,
    load_sem, block_send, meta_send, block_recv, meta_recv, best_send, best_recv,
):
    loads = [
        pltpu.make_async_copy(source, target, load_sem.at[i])
        for i, (source, target) in enumerate(
            ((emb_hbm, emb_ref), (cluster_hbm, cluster_ref), (dest_hbm, dest_ref))
        )
    ]
    for load in loads:
        load.start()
    rows = emb_ref.shape[0]
    half = rows // 2
    n_dest = dest_ref.shape[0]
    bank = lax.axis_index("bank")
    grp = lax.axis_index("grp")
    z = grp // 2
    x = grp % 2
    high = z // 2
    inner_z = 1 + high
    is_inner = z == inner_z
    mine = 2 * x + bank
    outer_add = jnp.where(is_inner, 0, 4)
    own = mine + outer_add

    barrier = pltpu.get_barrier_semaphore()
    for b in range(2):
        for g in range(8):

            @pl.when((bank != b) | (grp != g))
            def _():
                pl.semaphore_signal(
                    barrier, inc=1, device_id={"bank": b, "grp": g}, device_id_type=MESH
                )

    loads[0].wait()
    wide = emb_ref[...].astype(jnp.float32)
    scale = lax.rsqrt(jnp.sum(wide * wide, axis=1, keepdims=True) + small_eps)
    blocks[own] = (wide * scale).astype(jnp.bfloat16)

    pl.semaphore_wait(barrier, 15)

    def block_copy(index, slot, to_slot, part, to_bank, to_grp):
        span = pl.ds(part * half, half)
        return pltpu.make_async_remote_copy(
            src_ref=blocks.at[slot, span], dst_ref=blocks.at[to_slot, span],
            send_sem=block_send.at[index, part], recv_sem=block_recv.at[to_slot, part],
            device_id={"bank": to_bank, "grp": to_grp}, device_id_type=MESH,
        )

    def meta_copy(index, slot, to_slot, to_bank, to_grp):
        return pltpu.make_async_remote_copy(
            src_ref=meta.at[slot], dst_ref=meta.at[to_slot],
            send_sem=meta_send.at[index], recv_sem=meta_recv.at[to_slot],
            device_id={"bank": to_bank, "grp": to_grp}, device_id_type=MESH,
        )

    def sent(index, slot):
        meta_copy(index, slot, slot, 1 - bank, grp).wait_send()
        for part in range(2):
            block_copy(index, slot, slot, part, 1 - bank, grp).wait_send()

    def arrive_meta(slot):
        meta_copy(0, slot, slot, 1 - bank, grp).wait_recv()

    def arrive(slot, part):
        block_copy(0, slot, slot, part, 1 - bank, grp).wait_recv()

    def arrive_all(slot):
        arrive_meta(slot)
        arrive(slot, 0)
        arrive(slot, 1)

    x_grp = z * 2 + (1 - x)
    partner = (1 - bank, grp)
    beside = (bank, x_grp)

    @pl.when(jnp.logical_not(is_inner))
    def _():
        for part in range(2):
            block_copy(0, own, own, part, bank, inner_z * 2 + x).start()

    @pl.when(z == 1)
    def _():
        for part in range(2):
            block_copy(0, own, LOW, part, bank, grp + 2).start()

    @pl.when(is_inner)
    def _():
        for part in range(2):
            block_copy(1, own, own, part, *beside).start()
        for part in range(2):
            block_copy(2, own, own, part, *partner).start()

    loads[1].wait()
    loads[2].wait()
    row_id = lax.broadcasted_iota(jnp.int32, (dest_ref.shape[1], rows), 1)
    dest_columns = jnp.transpose(dest_ref[...].astype(jnp.float32)).astype(jnp.int32)
    slab_wide = jnp.full(row_id.shape, -1, jnp.int32)
    for d in range(n_dest):
        named = dest_columns[:, d : d + 1] == row_id
        slab_wide = jnp.maximum(slab_wide, jnp.where(named, d // (n_dest // 2), -1))
    slab = jnp.max(slab_wide, axis=0, keepdims=True)
    key = jnp.where(slab >= 0, cluster_ref[...] * 2 + slab, -1).astype(jnp.float32)
    own_meta[...] = jnp.broadcast_to(key, own_meta.shape)
    meta[own] = jnp.broadcast_to(key, own_meta.shape)
    best[...] = jnp.full(best.shape, -1.0, jnp.float32)

    @pl.when(jnp.logical_not(is_inner))
    def _():
        meta_copy(0, own, own, bank, inner_z * 2 + x).start()

    @pl.when(z == 1)
    def _():
        meta_copy(0, own, LOW, bank, grp + 2).start()

    @pl.when(is_inner)
    def _():
        meta_copy(1, own, own, *beside).start()
        meta_copy(2, own, own, *partner).start()

    def column(slot):
        wide_key = jnp.broadcast_to(meta[slot][:1], (128, rows))
        columns[slot] = jnp.transpose(wide_key)

    def slot_of(rel, outer):
        sx = (x + rel // 2) % 2
        sb = (bank + rel % 2) % 2
        slot = 2 * sx + sb + 4 * outer
        sz = inner_z if outer == 0 else 3 * high
        return slot, sb * 8 + sz * 2 + sx

    def scores_into(k_slot, q_slot, diagonal, k_rows=slice(None), q_rows=slice(None)):
        s = lax.dot_general(
            blocks[k_slot, k_rows], blocks[q_slot, q_rows], (((1,), (1,)), ((), ())),
            preferred_element_type=jnp.float32,
        )
        k_key = columns[k_slot, k_rows]
        q_key = meta[q_slot][:1]
        first = q_rows.start or 0
        for h in range(s.shape[1] // 128):
            from_s = slice(h * 128, (h + 1) * 128)
            part = slice(first + h * 128, first + (h + 1) * 128)
            allowed = k_key == q_key[:, part]
            if diagonal:
                k_id = lax.broadcasted_iota(jnp.int32, (rows, 128), 0)
                q_id = lax.broadcasted_iota(jnp.int32, (rows, 128), 1) + h * 128
                allowed = allowed & (k_id < q_id)
            kept = jnp.where(allowed, s[:, from_s], -1.0)
            top = jnp.max(kept.reshape(s.shape[0] // 8, 8, 128), axis=0)
            best[q_slot, :, part] = jnp.maximum(best[q_slot, :, part], top)

    def earlier(k, q):
        @pl.when(k[1] < q[1])
        def _():
            scores_into(k[0], q[0], False)

    def low_pair(which, rel, outer, part=None):
        low = LOW + which
        slot, shard = slot_of(rel, outer)
        low_shard = bank * 8 + (1 - which) * 2 + x
        if part is None:
            low_rows = slice(None)
        else:
            low_rows = slice(part * half, (part + 1) * half)

        @pl.when(low_shard < shard)
        def _():
            scores_into(low, slot, False, low_rows, slice(None))

        @pl.when(low_shard > shard)
        def _():
            scores_into(slot, low, False, slice(None), low_rows)

    @pl.when(is_inner)
    def _():
        in0, in1, in2, in3 = (slot_of(r, 0) for r in range(4))
        out0, out1, out2, out3 = (slot_of(r, 1) for r in range(4))
        column(in0[0])
        scores_into(in0[0], in0[0], True)
        arrive_all(in1[0])
        column(in1[0])
        earlier(in1, in0)

        arrive_meta(out0[0])

        @pl.when(z == 1)
        def _():
            meta_copy(3, out0[0], LOW + 1, bank, grp + 2).start()

        meta_copy(4, out0[0], out0[0], *beside).start()
        meta_copy(5, out0[0], out0[0], *partner).start()
        arrive_meta(in2[0])
        meta_copy(6, in2[0], in2[0], *partner).start()
        column(out0[0])
        column(in2[0])
        for part in range(2):
            arrive(out0[0], part)

            @pl.when(z == 1)
            def _():
                block_copy(3, out0[0], LOW + 1, part, bank, grp + 2).start()

            block_copy(4, out0[0], out0[0], part, *beside).start()
            block_copy(5, out0[0], out0[0], part, *partner).start()
            arrive(in2[0], part)
            block_copy(6, in2[0], in2[0], part, *partner).start()
        arrive_meta(out2[0])
        meta_copy(7, out2[0], out2[0], *partner).start()
        column(out2[0])
        scores_into(out0[0], out0[0], True)
        for k, q in ((out0, in0), (in0, out0), (in1, out0), (in2, in0), (in2, out0)):
            earlier(k, q)
        for k in (out1, in3):
            arrive_all(k[0])
            column(k[0])
            earlier(k, in0)
            earlier(k, out0)

        @pl.when(z == 2)
        def _():
            arrive_all(LOW)
            column(LOW)

            @pl.loop(0, 4)
            def _(rel):
                low_pair(0, rel, 0)

            @pl.loop(0, 2)
            def _(rel):
                low_pair(0, rel, 1)

            arrive_meta(LOW + 1)
            column(LOW + 1)

        for part in range(2):
            arrive(out2[0], part)
            block_copy(7, out2[0], out2[0], part, *partner).start()

            @pl.when(z == 2)
            def _():
                arrive(LOW + 1, part)

                @pl.loop(0, 4)
                def _(rel):
                    low_pair(1, rel, 0, part)

                @pl.loop(0, 2)
                def _(rel):
                    low_pair(1, rel, 1, part)

        for rel, k in ((2, out2), (3, out3)):
            if k is out3:
                arrive_all(k[0])
                column(k[0])
            earlier(k, in0)
            earlier(k, out0)

            @pl.when(z == 2)
            def _():
                low_pair(0, rel, 1)
                low_pair(1, rel, 1)

    def best_copy(index, slot, to, to_bank, to_grp):
        return pltpu.make_async_remote_copy(
            src_ref=best.at[slot], dst_ref=returned.at[to],
            send_sem=best_send.at[index], recv_sem=best_recv.at[to],
            device_id={"bank": to_bank, "grp": to_grp}, device_id_type=MESH,
        )

    @pl.when(z == 1)
    def _():
        best_copy(0, mine + 4, 0, bank, grp - 2).start()

    @pl.when(z == 2)
    def _():
        for rel in range(4):
            slot, _ = slot_of(rel, 0)
            to_bank = (bank + rel % 2) % 2
            to_x = (x + rel // 2) % 2
            best_copy(rel, slot + 4, mine, to_bank, 6 + to_x).start()
            if rel:
                best_copy(4 + rel, slot, mine, to_bank, 4 + to_x).start()

        @pl.when(bank == 1)
        def _():
            best_copy(4, LOW, 1, bank, grp - 2).start()
            best_copy(8, LOW + 1, 1, bank, grp - 4).start()

    def take(index):
        best_copy(0, own, index, 1 - bank, grp).wait_recv()
        best[own] = jnp.maximum(best[own], returned[index])

    def best_sent(index):
        best_copy(index, own, 0, 1 - bank, grp).wait_send()

    @pl.when(z == 0)
    def _():
        take(0)

    @pl.when((z < 2) & (bank == 1))
    def _():
        take(1)

    @pl.when(z >= 2)
    def _():
        for index in range(4):

            @pl.when((z == 3) | (mine != index))
            def _():
                take(index)

    top = jnp.max(best[own], axis=0, keepdims=True)
    out_ref[...] = jnp.where(own_meta[:1] >= 0, top, -1.0)

    @pl.when(jnp.logical_not(is_inner))
    def _():
        sent(0, own)

    @pl.when(is_inner)
    def _():
        for index in (1, 2, 4, 5, 6, 7):
            sent(index, own)

    @pl.when(z == 1)
    def _():
        sent(0, own)
        sent(3, own)
        best_sent(0)

    @pl.when(z == 2)
    def _():
        for index in (0, 1, 2, 3, 5, 6, 7):
            best_sent(index)

        @pl.when(bank == 1)
        def _():
            best_sent(4)
            best_sent(8)


def paired_on_device(embeddings, cluster_of, dest_list):
    rows, width = embeddings.shape
    dma = pltpu.SemaphoreType.DMA
    vmem = pl.BlockSpec(memory_space=pltpu.VMEM)
    result = pl.pallas_call(
        pair_kernel,
        out_shape=jax.ShapeDtypeStruct((1, rows), jnp.float32),
        in_specs=[pl.BlockSpec(memory_space=pltpu.HBM)] * 3,
        out_specs=vmem,
        scratch_shapes=[
            pltpu.VMEM((rows, width), jnp.bfloat16),
            pltpu.VMEM((1, rows), jnp.int32),
            pltpu.VMEM(dest_list.shape[1:], jnp.int32),
            pltpu.VMEM((10, rows, width), jnp.bfloat16),
            pltpu.VMEM((10, 8, rows), jnp.float32),
            pltpu.VMEM((10, rows, 128), jnp.float32),
            pltpu.VMEM((10, 8, rows), jnp.float32),
            pltpu.VMEM((4, 8, rows), jnp.float32),
            pltpu.VMEM((8, rows), jnp.float32),
            dma((3,)), dma((8, 2)), dma((8,)), dma((10, 2)), dma((10,)), dma((9,)), dma((4,)),
        ],
        compiler_params=pltpu.CompilerParams(
            collective_id=0, has_side_effects=True, vmem_limit_bytes=40 * 2**20
        ),
        cost_estimate=pl.CostEstimate(
            flops=16 * 2 * rows * rows * width, bytes_accessed=rows * width * 2, transcendentals=rows
        ),
    )(embeddings, cluster_of.reshape(1, rows), dest_list[0])
    return result.reshape(rows)


def solution(mesh):
    paired = mesh.shape["bank"] == 2 and mesh.shape["grp"] == 8
    return jax.shard_map(
        paired_on_device if paired else routed_on_device,
        mesh=mesh,
        in_specs=(
            P(("dom", "bank", "grp"), None),
            P(("dom", "bank", "grp")),
            P(("dom", "bank", "grp"), None, None),
        ),
        out_specs=P(("dom", "bank", "grp")),
        check_vma=False,
    )
```

```python
import functools
import jax
import jax.numpy as jnp
from jax import lax
from jax.experimental import pallas as pl
from jax.experimental.pallas import tpu as pltpu
from jax.sharding import PartitionSpec as P

small_eps = 1e-06
MESH = pl.DeviceIdType.MESH


def masked_scores(query_rows, query_cluster, other_rows, other_cluster):
    scores = lax.dot_general(
        query_rows, other_rows, (((1,), (1,)), ((), ())), preferred_element_type=jnp.float32
    )
    matching = query_cluster[:, None] == other_cluster[None, :]
    return (scores, matching)


def routed_on_device(embeddings, cluster_of, dest_list):
    rows_dev = embeddings.shape[0]
    width = embeddings.shape[1]
    devices_part = dest_list.shape[1]
    capacity = dest_list.shape[2]
    source = lax.axis_index(("bank", "grp"))
    widened = embeddings.astype(jnp.float32)
    unit_rows = (
        widened * lax.rsqrt(jnp.sum(widened * widened, axis=1, keepdims=True) + small_eps)
    ).astype(jnp.bfloat16)
    slot_rows = dest_list[0]
    is_live = slot_rows >= 0
    safe_rows = jnp.where(is_live, slot_rows, 0)
    outgoing = jnp.take(unit_rows, safe_rows.reshape(-1), axis=0).reshape(
        devices_part, capacity, width
    )
    out_cluster = jnp.where(is_live, jnp.take(cluster_of, safe_rows), -1)
    out_crawl = jnp.where(is_live, source * rows_dev + safe_rows, -1)
    arrived, in_cluster, in_crawl = (
        lax.all_to_all(outgoing, ("bank", "grp"), split_axis=0, concat_axis=0, tiled=True),
        lax.all_to_all(out_cluster, ("bank", "grp"), split_axis=0, concat_axis=0, tiled=True),
        lax.all_to_all(out_crawl, ("bank", "grp"), split_axis=0, concat_axis=0, tiled=True),
    )
    flat_cluster = in_cluster.reshape(-1)
    flat_crawl = in_crawl.reshape(-1)
    present = flat_cluster >= 0
    position = jnp.cumsum(present.astype(jnp.int32)) - 1
    chosen = (position[None, :] == jnp.arange(rows_dev, dtype=jnp.int32)[:, None]) & present[
        None, :
    ]
    key_rows = jnp.dot(
        chosen.astype(jnp.bfloat16), arrived.reshape(-1, width), preferred_element_type=jnp.float32
    ).astype(jnp.bfloat16)
    key_cluster = jnp.sum(jnp.where(chosen, flat_cluster[None, :], 0), axis=1)
    key_crawl = jnp.sum(jnp.where(chosen, flat_crawl[None, :], 0), axis=1)
    floor_value = jnp.full((rows_dev,), -1.0, jnp.float32)
    scores, matching = masked_scores(
        key_rows,
        key_cluster,
        lax.all_gather(key_rows, "grp", axis=0, tiled=True),
        lax.all_gather(key_cluster, "grp", axis=0, tiled=True),
    )
    earlier = matching & (
        lax.all_gather(key_crawl, "grp", axis=0, tiled=True)[None, :] < key_crawl[:, None]
    )
    best_sim = jnp.maximum(floor_value, jnp.max(jnp.where(earlier, scores, -1.0), axis=1))
    slot_best = jnp.where(
        present, jnp.take(best_sim, jnp.clip(position, 0, rows_dev - 1)), -1.0
    ).reshape(devices_part, capacity)
    returned_best = lax.all_to_all(
        slot_best, ("bank", "grp"), split_axis=0, concat_axis=0, tiled=True
    )
    result = (
        jnp.full((rows_dev,), -1.0, jnp.float32)
        .at[safe_rows.reshape(-1)]
        .max(jnp.where(is_live, returned_best, -1.0).reshape(-1))
    )
    return result


LOW = 8


def pair_kernel(
    emb_hbm, cluster_hbm, dest_hbm, out_ref,
    emb_ref, cluster_ref, dest_ref, blocks, meta, columns, best, returned, own_meta,
    load_sem, ready_sem, block_send, meta_send, block_recv, meta_recv, best_send, best_recv,
):
    loads = [
        pltpu.make_async_copy(source, target, load_sem.at[i])
        for i, (source, target) in enumerate(
            ((emb_hbm, emb_ref), (cluster_hbm, cluster_ref), (dest_hbm, dest_ref))
        )
    ]
    for load in loads:
        load.start()
    rows = emb_ref.shape[0]
    half = rows // 2
    n_dest = dest_ref.shape[0]
    bank = lax.axis_index("bank")
    grp = lax.axis_index("grp")
    z = grp // 2
    x = grp % 2
    high = z // 2
    inner_z = 1 + high
    is_inner = z == inner_z
    mine = 2 * x + bank
    outer_add = jnp.where(is_inner, 0, 4)
    own = mine + outer_add

    barrier = pltpu.get_barrier_semaphore()
    x_grp = z * 2 + (1 - x)
    partner = (1 - bank, grp)
    beside = (bank, x_grp)

    def greet(to_bank, to_grp, sem=barrier):
        pl.semaphore_signal(
            sem, inc=1, device_id={"bank": to_bank, "grp": to_grp}, device_id_type=MESH
        )

    greet(*beside)

    @pl.when(z == 0)
    def _():
        greet(bank, grp + 2)

    @pl.when((z == 0) & (bank == 1))
    def _():
        greet(bank, grp + 4)

    @pl.when(z == 1)
    def _():
        greet(*partner)
        greet(bank, grp - 2)

    @pl.when((z == 1) & (bank == 1))
    def _():
        greet(bank, grp + 2)

    @pl.when(z == 2)
    def _():
        greet(*partner)
        greet(1 - bank, x_grp)
        greet(bank, grp - 2)
        for b in range(2):
            for other_x in range(2):
                greet(b, 6 + other_x)

    loads[0].wait()
    wide = emb_ref[...].astype(jnp.float32)
    scale = lax.rsqrt(jnp.sum(wide * wide, axis=1, keepdims=True) + small_eps)
    blocks[own] = (wide * scale).astype(jnp.bfloat16)

    @pl.when(z == 0)
    def _():
        pl.semaphore_wait(barrier, 2)

    @pl.when(z == 1)
    def _():
        pl.semaphore_wait(barrier, 4)

    @pl.when((z == 2) & (bank == 0))
    def _():
        pl.semaphore_wait(barrier, 3)

    @pl.when((z == 2) & (bank == 1))
    def _():
        pl.semaphore_wait(barrier, 5)

    @pl.when(z == 3)
    def _():
        pl.semaphore_wait(barrier, 5)
        for b in range(2):
            for other_x in range(2):
                greet(b, 4 + other_x, ready_sem)

    def block_copy(index, slot, to_slot, part, to_bank, to_grp):
        span = pl.ds(part * half, half)
        return pltpu.make_async_remote_copy(
            src_ref=blocks.at[slot, span], dst_ref=blocks.at[to_slot, span],
            send_sem=block_send.at[index, part], recv_sem=block_recv.at[to_slot, part],
            device_id={"bank": to_bank, "grp": to_grp}, device_id_type=MESH,
        )

    def meta_copy(index, slot, to_slot, to_bank, to_grp):
        return pltpu.make_async_remote_copy(
            src_ref=meta.at[slot], dst_ref=meta.at[to_slot],
            send_sem=meta_send.at[index], recv_sem=meta_recv.at[to_slot],
            device_id={"bank": to_bank, "grp": to_grp}, device_id_type=MESH,
        )

    def sent(index, slot, parts=(0, 1), with_meta=True):
        if with_meta:
            meta_copy(index, slot, slot, 1 - bank, grp).wait_send()
        for part in parts:
            block_copy(index, slot, slot, part, 1 - bank, grp).wait_send()

    def arrive_meta(slot):
        meta_copy(0, slot, slot, 1 - bank, grp).wait_recv()

    def arrive(slot, part):
        block_copy(0, slot, slot, part, 1 - bank, grp).wait_recv()

    def arrive_all(slot):
        arrive_meta(slot)
        arrive(slot, 0)
        arrive(slot, 1)

    @pl.when(jnp.logical_not(is_inner))
    def _():
        for part in range(2):
            block_copy(0, own, own, part, bank, inner_z * 2 + x).start()
        block_copy(1, own, own, 1, *beside).start()

    @pl.when(z == 1)
    def _():
        for part in range(2):
            block_copy(0, own, LOW, part, bank, grp + 2).start()

    @pl.when(is_inner)
    def _():
        for part in range(2):
            block_copy(1, own, own, part, *beside).start()
        for part in range(2):
            block_copy(2, own, own, part, *partner).start()

    loads[1].wait()
    loads[2].wait()
    row_id = lax.broadcasted_iota(jnp.int32, (dest_ref.shape[1], rows), 1)
    dest_columns = jnp.transpose(dest_ref[...].astype(jnp.float32)).astype(jnp.int32)
    slab_wide = jnp.full(row_id.shape, -1, jnp.int32)
    for d in range(n_dest):
        named = dest_columns[:, d : d + 1] == row_id
        slab_wide = jnp.maximum(slab_wide, jnp.where(named, d // (n_dest // 2), -1))
    slab = jnp.max(slab_wide, axis=0, keepdims=True)
    key = jnp.where(slab >= 0, cluster_ref[...] * 2 + slab, -1).astype(jnp.float32)
    own_meta[...] = jnp.broadcast_to(key, own_meta.shape)
    meta[own] = jnp.broadcast_to(key, own_meta.shape)
    best[...] = jnp.full(best.shape, -1.0, jnp.float32)

    @pl.when(jnp.logical_not(is_inner))
    def _():
        meta_copy(0, own, own, bank, inner_z * 2 + x).start()

    @pl.when(z == 1)
    def _():
        meta_copy(0, own, LOW, bank, grp + 2).start()

    @pl.when(is_inner)
    def _():
        meta_copy(1, own, own, *beside).start()
        meta_copy(2, own, own, *partner).start()

    def column(slot):
        wide_key = jnp.broadcast_to(meta[slot][:1], (128, rows))
        columns[slot] = jnp.transpose(wide_key)

    def slot_of(rel, outer):
        sx = (x + rel // 2) % 2
        sb = (bank + rel % 2) % 2
        slot = 2 * sx + sb + 4 * outer
        sz = inner_z if outer == 0 else 3 * high
        return slot, sb * 8 + sz * 2 + sx

    def scores_into(k_slot, q_slot, diagonal, k_rows=slice(None), q_rows=slice(None)):
        s = lax.dot_general(
            blocks[k_slot, k_rows], blocks[q_slot, q_rows], (((1,), (1,)), ((), ())),
            preferred_element_type=jnp.float32,
        )
        k_key = columns[k_slot, k_rows]
        q_key = meta[q_slot][:1]
        first = q_rows.start or 0
        for h in range(s.shape[1] // 128):
            from_s = slice(h * 128, (h + 1) * 128)
            part = slice(first + h * 128, first + (h + 1) * 128)
            allowed = k_key == q_key[:, part]
            if diagonal:
                k_id = lax.broadcasted_iota(jnp.int32, (rows, 128), 0)
                q_id = lax.broadcasted_iota(jnp.int32, (rows, 128), 1) + h * 128
                allowed = allowed & (k_id < q_id)
            kept = jnp.where(allowed, s[:, from_s], -1.0)
            top = jnp.max(kept.reshape(s.shape[0] // 8, 8, 128), axis=0)
            best[q_slot, :, part] = jnp.maximum(best[q_slot, :, part], top)

    def earlier(k, q):
        @pl.when(k[1] < q[1])
        def _():
            scores_into(k[0], q[0], False)

    def low_pair(which, rel, outer, part=None):
        low = LOW + which
        slot, shard = slot_of(rel, outer)
        low_shard = bank * 8 + (1 - which) * 2 + x
        if part is None:
            low_rows = slice(None)
        else:
            low_rows = slice(part * half, (part + 1) * half)

        @pl.when(low_shard < shard)
        def _():
            scores_into(low, slot, False, low_rows, slice(None))

        @pl.when(low_shard > shard)
        def _():
            scores_into(slot, low, False, slice(None), low_rows)

    @pl.when(is_inner)
    def _():
        in0, in1, in2, in3 = (slot_of(r, 0) for r in range(4))
        out0, out1, out2, out3 = (slot_of(r, 1) for r in range(4))
        column(in0[0])
        scores_into(in0[0], in0[0], True)
        arrive_all(in1[0])
        column(in1[0])
        earlier(in1, in0)

        arrive_meta(out0[0])

        @pl.when(z == 1)
        def _():
            meta_copy(3, out0[0], LOW + 1, bank, grp + 2).start()

        meta_copy(4, out0[0], out0[0], *beside).start()
        meta_copy(5, out0[0], out0[0], *partner).start()
        arrive_meta(in2[0])
        meta_copy(6, in2[0], in2[0], *partner).start()
        column(out0[0])
        column(in2[0])
        for part in range(2):
            arrive(out0[0], part)

            @pl.when(z == 1)
            def _():
                block_copy(3, out0[0], LOW + 1, part, bank, grp + 2).start()

            if part == 0:
                block_copy(4, out0[0], out0[0], part, *beside).start()
            block_copy(5, out0[0], out0[0], part, *partner).start()
            arrive(in2[0], part)
            block_copy(6, in2[0], in2[0], part, *partner).start()
        arrive_meta(out2[0])
        meta_copy(7, out2[0], out2[0], *partner).start()
        column(out2[0])
        scores_into(out0[0], out0[0], True)
        for k, q in ((out0, in0), (in0, out0), (in1, out0), (in2, in0), (in2, out0)):
            earlier(k, q)
        for k in (out1, in3):
            arrive_all(k[0])
            column(k[0])
            earlier(k, in0)
            earlier(k, out0)

        @pl.when(z == 2)
        def _():
            arrive_all(LOW)
            column(LOW)

            @pl.loop(0, 4)
            def _(rel):
                low_pair(0, rel, 0)

            @pl.loop(0, 2)
            def _(rel):
                low_pair(0, rel, 1)

            arrive_meta(LOW + 1)
            column(LOW + 1)

        for part in range(2):
            arrive(out2[0], part)
            block_copy(7, out2[0], out2[0], part, *partner).start()

            @pl.when(z == 2)
            def _():
                arrive(LOW + 1, part)

                @pl.loop(0, 4)
                def _(rel):
                    low_pair(1, rel, 0, part)

                @pl.loop(0, 2)
                def _(rel):
                    low_pair(1, rel, 1, part)

        for rel, k in ((2, out2), (3, out3)):
            if k is out3:
                arrive_all(k[0])
                column(k[0])
            earlier(k, in0)
            earlier(k, out0)

            @pl.when(z == 2)
            def _():
                low_pair(0, rel, 1)
                low_pair(1, rel, 1)

    @pl.when(jnp.logical_not(is_inner))
    def _():
        other = 2 * (1 - x) + bank + 4
        arrive(other, 1)
        block_copy(2, other, other, 1, bank, inner_z * 2 + x).start()

    def best_copy(index, slot, to, to_bank, to_grp):
        return pltpu.make_async_remote_copy(
            src_ref=best.at[slot], dst_ref=returned.at[to],
            send_sem=best_send.at[index], recv_sem=best_recv.at[to],
            device_id={"bank": to_bank, "grp": to_grp}, device_id_type=MESH,
        )

    @pl.when(z == 1)
    def _():
        best_copy(0, mine + 4, 0, bank, grp - 2).start()

    @pl.when(z == 2)
    def _():
        pl.semaphore_wait(ready_sem, 4)
        for rel in range(4):
            slot, _ = slot_of(rel, 0)
            to_bank = (bank + rel % 2) % 2
            to_x = (x + rel // 2) % 2
            best_copy(rel, slot + 4, mine, to_bank, 6 + to_x).start()
            if rel:
                best_copy(4 + rel, slot, mine, to_bank, 4 + to_x).start()

        @pl.when(bank == 1)
        def _():
            best_copy(4, LOW, 1, bank, grp - 2).start()
            best_copy(8, LOW + 1, 1, bank, grp - 4).start()

    def take(index):
        best_copy(0, own, index, 1 - bank, grp).wait_recv()
        best[own] = jnp.maximum(best[own], returned[index])

    def best_sent(index):
        best_copy(index, own, 0, 1 - bank, grp).wait_send()

    @pl.when(z == 0)
    def _():
        take(0)

    @pl.when((z < 2) & (bank == 1))
    def _():
        take(1)

    @pl.when(z >= 2)
    def _():
        for index in range(4):

            @pl.when((z == 3) | (mine != index))
            def _():
                take(index)

    top = jnp.max(best[own], axis=0, keepdims=True)
    out_ref[...] = jnp.where(own_meta[:1] >= 0, top, -1.0)

    @pl.when(jnp.logical_not(is_inner))
    def _():
        sent(0, own)
        for index in (1, 2):
            sent(index, own, (1,), False)

    @pl.when(is_inner)
    def _():
        for index in (1, 2, 5, 6, 7):
            sent(index, own)
        sent(4, own, (0,))

    @pl.when(z == 1)
    def _():
        sent(0, own)
        sent(3, own)
        best_sent(0)

    @pl.when(z == 2)
    def _():
        for index in (0, 1, 2, 3, 5, 6, 7):
            best_sent(index)

        @pl.when(bank == 1)
        def _():
            best_sent(4)
            best_sent(8)


def paired_on_device(embeddings, cluster_of, dest_list):
    rows, width = embeddings.shape
    dma = pltpu.SemaphoreType.DMA
    vmem = pl.BlockSpec(memory_space=pltpu.VMEM)
    result = pl.pallas_call(
        pair_kernel,
        out_shape=jax.ShapeDtypeStruct((1, rows), jnp.float32),
        in_specs=[pl.BlockSpec(memory_space=pltpu.HBM)] * 3,
        out_specs=vmem,
        scratch_shapes=[
            pltpu.VMEM((rows, width), jnp.bfloat16),
            pltpu.VMEM((1, rows), jnp.int32),
            pltpu.VMEM(dest_list.shape[1:], jnp.int32),
            pltpu.VMEM((10, rows, width), jnp.bfloat16),
            pltpu.VMEM((10, 8, rows), jnp.float32),
            pltpu.VMEM((10, rows, 128), jnp.float32),
            pltpu.VMEM((10, 8, rows), jnp.float32),
            pltpu.VMEM((4, 8, rows), jnp.float32),
            pltpu.VMEM((8, rows), jnp.float32),
            dma((3,)), pltpu.SemaphoreType.REGULAR, dma((8, 2)), dma((8,)), dma((10, 2)), dma((10,)), dma((9,)), dma((4,)),
        ],
        compiler_params=pltpu.CompilerParams(
            collective_id=0, has_side_effects=True, vmem_limit_bytes=60 * 2**20
        ),
        cost_estimate=pl.CostEstimate(
            flops=16 * 2 * rows * rows * width, bytes_accessed=rows * width * 2, transcendentals=rows
        ),
    )(embeddings, cluster_of.reshape(1, rows), dest_list[0])
    return result.reshape(rows)


def solution(mesh):
    paired = mesh.shape["bank"] == 2 and mesh.shape["grp"] == 8
    return jax.shard_map(
        paired_on_device if paired else routed_on_device,
        mesh=mesh,
        in_specs=(
            P(("dom", "bank", "grp"), None),
            P(("dom", "bank", "grp")),
            P(("dom", "bank", "grp"), None, None),
        ),
        out_specs=P(("dom", "bank", "grp")),
        check_vma=False,
    )
```

```python
import functools
import jax
import jax.numpy as jnp
from jax import lax
from jax.experimental import pallas as pl
from jax.experimental.pallas import tpu as pltpu
from jax.sharding import PartitionSpec as P

small_eps = 1e-06
MESH = pl.DeviceIdType.MESH


def masked_scores(query_rows, query_cluster, other_rows, other_cluster):
    scores = lax.dot_general(
        query_rows, other_rows, (((1,), (1,)), ((), ())), preferred_element_type=jnp.float32
    )
    matching = query_cluster[:, None] == other_cluster[None, :]
    return (scores, matching)


def routed_on_device(embeddings, cluster_of, dest_list):
    rows_dev = embeddings.shape[0]
    width = embeddings.shape[1]
    devices_part = dest_list.shape[1]
    capacity = dest_list.shape[2]
    source = lax.axis_index(("bank", "grp"))
    widened = embeddings.astype(jnp.float32)
    unit_rows = (
        widened * lax.rsqrt(jnp.sum(widened * widened, axis=1, keepdims=True) + small_eps)
    ).astype(jnp.bfloat16)
    slot_rows = dest_list[0]
    is_live = slot_rows >= 0
    safe_rows = jnp.where(is_live, slot_rows, 0)
    outgoing = jnp.take(unit_rows, safe_rows.reshape(-1), axis=0).reshape(
        devices_part, capacity, width
    )
    out_cluster = jnp.where(is_live, jnp.take(cluster_of, safe_rows), -1)
    out_crawl = jnp.where(is_live, source * rows_dev + safe_rows, -1)
    arrived, in_cluster, in_crawl = (
        lax.all_to_all(outgoing, ("bank", "grp"), split_axis=0, concat_axis=0, tiled=True),
        lax.all_to_all(out_cluster, ("bank", "grp"), split_axis=0, concat_axis=0, tiled=True),
        lax.all_to_all(out_crawl, ("bank", "grp"), split_axis=0, concat_axis=0, tiled=True),
    )
    flat_cluster = in_cluster.reshape(-1)
    flat_crawl = in_crawl.reshape(-1)
    present = flat_cluster >= 0
    position = jnp.cumsum(present.astype(jnp.int32)) - 1
    chosen = (position[None, :] == jnp.arange(rows_dev, dtype=jnp.int32)[:, None]) & present[
        None, :
    ]
    key_rows = jnp.dot(
        chosen.astype(jnp.bfloat16), arrived.reshape(-1, width), preferred_element_type=jnp.float32
    ).astype(jnp.bfloat16)
    key_cluster = jnp.sum(jnp.where(chosen, flat_cluster[None, :], 0), axis=1)
    key_crawl = jnp.sum(jnp.where(chosen, flat_crawl[None, :], 0), axis=1)
    floor_value = jnp.full((rows_dev,), -1.0, jnp.float32)
    scores, matching = masked_scores(
        key_rows,
        key_cluster,
        lax.all_gather(key_rows, "grp", axis=0, tiled=True),
        lax.all_gather(key_cluster, "grp", axis=0, tiled=True),
    )
    earlier = matching & (
        lax.all_gather(key_crawl, "grp", axis=0, tiled=True)[None, :] < key_crawl[:, None]
    )
    best_sim = jnp.maximum(floor_value, jnp.max(jnp.where(earlier, scores, -1.0), axis=1))
    slot_best = jnp.where(
        present, jnp.take(best_sim, jnp.clip(position, 0, rows_dev - 1)), -1.0
    ).reshape(devices_part, capacity)
    returned_best = lax.all_to_all(
        slot_best, ("bank", "grp"), split_axis=0, concat_axis=0, tiled=True
    )
    result = (
        jnp.full((rows_dev,), -1.0, jnp.float32)
        .at[safe_rows.reshape(-1)]
        .max(jnp.where(is_live, returned_best, -1.0).reshape(-1))
    )
    return result


LOW = 8


def pair_kernel(
    emb_hbm, cluster_hbm, dest_hbm, out_ref,
    emb_ref, cluster_ref, dest_ref, blocks, meta, columns, best, returned, own_meta,
    load_sem, ready_sem, block_send, meta_send, block_recv, meta_recv, best_send, best_recv,
):
    loads = [
        pltpu.make_async_copy(source, target, load_sem.at[i])
        for i, (source, target) in enumerate(
            ((emb_hbm, emb_ref), (cluster_hbm, cluster_ref), (dest_hbm, dest_ref))
        )
    ]
    for load in loads:
        load.start()
    rows = emb_ref.shape[0]
    half = rows // 2
    n_dest = dest_ref.shape[0]
    bank = lax.axis_index("bank")
    grp = lax.axis_index("grp")
    z = grp // 2
    x = grp % 2
    high = z // 2
    inner_z = 1 + high
    is_inner = z == inner_z
    mine = 2 * x + bank
    outer_add = jnp.where(is_inner, 0, 4)
    own = mine + outer_add

    barrier = pltpu.get_barrier_semaphore()
    x_grp = z * 2 + (1 - x)
    partner = (1 - bank, grp)
    beside = (bank, x_grp)

    def greet(to_bank, to_grp, sem=barrier):
        pl.semaphore_signal(
            sem, inc=1, device_id={"bank": to_bank, "grp": to_grp}, device_id_type=MESH
        )

    greet(*beside)

    @pl.when(z == 0)
    def _():
        greet(bank, grp + 2)

    @pl.when((z == 0) & (bank == 1))
    def _():
        greet(bank, grp + 4)

    @pl.when(z == 1)
    def _():
        greet(*partner)
        greet(bank, grp - 2)

    @pl.when((z == 1) & (bank == 1))
    def _():
        greet(bank, grp + 2)

    @pl.when(z == 2)
    def _():
        greet(*partner)
        greet(1 - bank, x_grp)
        greet(bank, grp - 2)
        for b in range(2):
            for other_x in range(2):
                greet(b, 6 + other_x)

    loads[0].wait()
    wide = emb_ref[...].astype(jnp.float32)
    scale = lax.rsqrt(jnp.sum(wide * wide, axis=1, keepdims=True) + small_eps)
    blocks[own] = (wide * scale).astype(jnp.bfloat16)

    @pl.when(z == 0)
    def _():
        pl.semaphore_wait(barrier, 2)

    @pl.when(z == 1)
    def _():
        pl.semaphore_wait(barrier, 4)

    @pl.when((z == 2) & (bank == 0))
    def _():
        pl.semaphore_wait(barrier, 3)

    @pl.when((z == 2) & (bank == 1))
    def _():
        pl.semaphore_wait(barrier, 5)

    @pl.when(z == 3)
    def _():
        pl.semaphore_wait(barrier, 5)
        for b in range(2):
            for other_x in range(2):
                greet(b, 4 + other_x, ready_sem)

    def block_copy(index, slot, to_slot, part, to_bank, to_grp):
        span = pl.ds(part * half, half)
        return pltpu.make_async_remote_copy(
            src_ref=blocks.at[slot, span], dst_ref=blocks.at[to_slot, span],
            send_sem=block_send.at[index, part], recv_sem=block_recv.at[to_slot, part],
            device_id={"bank": to_bank, "grp": to_grp}, device_id_type=MESH,
        )

    def meta_copy(index, slot, to_slot, to_bank, to_grp):
        return pltpu.make_async_remote_copy(
            src_ref=meta.at[slot], dst_ref=meta.at[to_slot],
            send_sem=meta_send.at[index], recv_sem=meta_recv.at[to_slot],
            device_id={"bank": to_bank, "grp": to_grp}, device_id_type=MESH,
        )

    def sent(index, slot, parts=(0, 1), with_meta=True):
        if with_meta:
            meta_copy(index, slot, slot, 1 - bank, grp).wait_send()
        for part in parts:
            block_copy(index, slot, slot, part, 1 - bank, grp).wait_send()

    def arrive_meta(slot):
        meta_copy(0, slot, slot, 1 - bank, grp).wait_recv()

    def arrive(slot, part):
        block_copy(0, slot, slot, part, 1 - bank, grp).wait_recv()

    def arrive_all(slot):
        arrive_meta(slot)
        arrive(slot, 0)
        arrive(slot, 1)

    @pl.when(jnp.logical_not(is_inner))
    def _():
        for part in range(2):
            block_copy(0, own, own, part, bank, inner_z * 2 + x).start()
        block_copy(1, own, own, 1, *beside).start()

    @pl.when(z == 1)
    def _():
        for part in range(2):
            block_copy(0, own, LOW, part, bank, grp + 2).start()

    @pl.when(is_inner)
    def _():
        for part in range(2):
            block_copy(1, own, own, part, *beside).start()
        for part in range(2):
            block_copy(2, own, own, part, *partner).start()

    loads[1].wait()
    loads[2].wait()
    row_id = lax.broadcasted_iota(jnp.int32, (dest_ref.shape[1], rows), 1)
    dest_columns = jnp.transpose(dest_ref[...].astype(jnp.float32)).astype(jnp.int32)
    slab_wide = jnp.full(row_id.shape, -1, jnp.int32)
    for d in range(n_dest):
        named = dest_columns[:, d : d + 1] == row_id
        slab_wide = jnp.maximum(slab_wide, jnp.where(named, d // (n_dest // 2), -1))
    slab = jnp.max(slab_wide, axis=0, keepdims=True)
    key = jnp.where(slab >= 0, cluster_ref[...] * 2 + slab, -1).astype(jnp.float32)
    own_meta[...] = jnp.broadcast_to(key, own_meta.shape)
    meta[own] = jnp.broadcast_to(key, own_meta.shape)
    best[...] = jnp.full(best.shape, -1.0, jnp.float32)

    @pl.when(jnp.logical_not(is_inner))
    def _():
        meta_copy(0, own, own, bank, inner_z * 2 + x).start()

    @pl.when(z == 1)
    def _():
        meta_copy(0, own, LOW, bank, grp + 2).start()

    @pl.when(is_inner)
    def _():
        meta_copy(1, own, own, *beside).start()
        meta_copy(2, own, own, *partner).start()

    def column(slot):
        wide_key = jnp.broadcast_to(meta[slot][:1], (128, rows))
        columns[slot] = jnp.transpose(wide_key)

    def slot_of(rel, outer):
        sx = (x + rel // 2) % 2
        sb = (bank + rel % 2) % 2
        slot = 2 * sx + sb + 4 * outer
        sz = inner_z if outer == 0 else 3 * high
        return slot, sb * 8 + sz * 2 + sx

    def scores_into(k_slot, q_slot, diagonal, k_rows=slice(None), q_rows=slice(None)):
        s = lax.dot_general(
            blocks[k_slot, k_rows], blocks[q_slot, q_rows], (((1,), (1,)), ((), ())),
            preferred_element_type=jnp.float32,
        )
        k_key = columns[k_slot, k_rows]
        q_key = meta[q_slot][:1]
        first = q_rows.start or 0
        for h in range(s.shape[1] // 128):
            from_s = slice(h * 128, (h + 1) * 128)
            part = slice(first + h * 128, first + (h + 1) * 128)
            allowed = k_key == q_key[:, part]
            if diagonal:
                k_id = lax.broadcasted_iota(jnp.int32, (rows, 128), 0)
                q_id = lax.broadcasted_iota(jnp.int32, (rows, 128), 1) + h * 128
                allowed = allowed & (k_id < q_id)
            kept = jnp.where(allowed, s[:, from_s], -1.0)
            top = jnp.max(kept.reshape(s.shape[0] // 8, 8, 128), axis=0)
            best[q_slot, :, part] = jnp.maximum(best[q_slot, :, part], top)

    def earlier(k, q):
        @pl.when(k[1] < q[1])
        def _():
            scores_into(k[0], q[0], False)

    def low_pair(which, rel, outer, part=None):
        low = LOW + which
        slot, shard = slot_of(rel, outer)
        low_shard = bank * 8 + (1 - which) * 2 + x
        if part is None:
            low_rows = slice(None)
        else:
            low_rows = slice(part * half, (part + 1) * half)

        @pl.when(low_shard < shard)
        def _():
            scores_into(low, slot, False, low_rows, slice(None))

        @pl.when(low_shard > shard)
        def _():
            scores_into(slot, low, False, slice(None), low_rows)

    @pl.when(is_inner)
    def _():
        in0, in1, in2, in3 = (slot_of(r, 0) for r in range(4))
        out0, out1, out2, out3 = (slot_of(r, 1) for r in range(4))
        column(in0[0])
        scores_into(in0[0], in0[0], True)
        arrive_all(in1[0])
        column(in1[0])
        earlier(in1, in0)

        arrive_meta(out0[0])

        @pl.when(z == 1)
        def _():
            meta_copy(3, out0[0], LOW + 1, bank, grp + 2).start()

        meta_copy(4, out0[0], out0[0], *beside).start()
        meta_copy(5, out0[0], out0[0], *partner).start()
        arrive_meta(in2[0])
        meta_copy(6, in2[0], in2[0], *partner).start()
        column(out0[0])
        column(in2[0])
        for part in range(2):
            arrive(out0[0], part)

            @pl.when(z == 1)
            def _():
                block_copy(3, out0[0], LOW + 1, part, bank, grp + 2).start()

            if part == 0:
                block_copy(4, out0[0], out0[0], part, *beside).start()
            block_copy(5, out0[0], out0[0], part, *partner).start()
            arrive(in2[0], part)
            block_copy(6, in2[0], in2[0], part, *partner).start()
        arrive_meta(out2[0])
        meta_copy(7, out2[0], out2[0], *partner).start()
        column(out2[0])
        scores_into(out0[0], out0[0], True)
        for k, q in ((out0, in0), (in0, out0), (in1, out0), (in2, in0), (in2, out0)):
            earlier(k, q)
        for k in (out1, in3):
            arrive_all(k[0])
            column(k[0])
            earlier(k, in0)
            earlier(k, out0)

        @pl.when(z == 2)
        def _():
            arrive_all(LOW)
            column(LOW)

            @pl.loop(0, 4)
            def _(rel):
                low_pair(0, rel, 0)

            @pl.loop(0, 2)
            def _(rel):
                low_pair(0, rel, 1)

            arrive_meta(LOW + 1)
            column(LOW + 1)

        for part in range(2):
            arrive(out2[0], part)
            block_copy(7, out2[0], out2[0], part, *partner).start()

        @pl.when(z == 2)
        def _():
            for part in range(2):
                arrive(LOW + 1, part)

            @pl.loop(0, 4)
            def _(rel):
                low_pair(1, rel, 0)

            @pl.loop(0, 2)
            def _(rel):
                low_pair(1, rel, 1)

        for rel, k in ((2, out2), (3, out3)):
            if k is out3:
                arrive_all(k[0])
                column(k[0])
            earlier(k, in0)
            earlier(k, out0)

            @pl.when(z == 2)
            def _():
                low_pair(0, rel, 1)
                low_pair(1, rel, 1)

    @pl.when(jnp.logical_not(is_inner))
    def _():
        other = 2 * (1 - x) + bank + 4
        arrive(other, 1)
        block_copy(2, other, other, 1, bank, inner_z * 2 + x).start()

    def best_copy(index, slot, to, to_bank, to_grp):
        return pltpu.make_async_remote_copy(
            src_ref=best.at[slot], dst_ref=returned.at[to],
            send_sem=best_send.at[index], recv_sem=best_recv.at[to],
            device_id={"bank": to_bank, "grp": to_grp}, device_id_type=MESH,
        )

    @pl.when(z == 1)
    def _():
        best_copy(0, mine + 4, 0, bank, grp - 2).start()

    @pl.when(z == 2)
    def _():
        pl.semaphore_wait(ready_sem, 4)
        for rel in range(4):
            slot, _ = slot_of(rel, 0)
            to_bank = (bank + rel % 2) % 2
            to_x = (x + rel // 2) % 2
            best_copy(rel, slot + 4, mine, to_bank, 6 + to_x).start()
            if rel:
                best_copy(4 + rel, slot, mine, to_bank, 4 + to_x).start()

        @pl.when(bank == 1)
        def _():
            best_copy(4, LOW, 1, bank, grp - 2).start()
            best_copy(8, LOW + 1, 1, bank, grp - 4).start()

    def take(index):
        best_copy(0, own, index, 1 - bank, grp).wait_recv()
        best[own] = jnp.maximum(best[own], returned[index])

    def best_sent(index):
        best_copy(index, own, 0, 1 - bank, grp).wait_send()

    @pl.when(z == 0)
    def _():
        take(0)

    @pl.when((z < 2) & (bank == 1))
    def _():
        take(1)

    @pl.when(z >= 2)
    def _():
        for index in range(4):

            @pl.when((z == 3) | (mine != index))
            def _():
                take(index)

    top = jnp.max(best[own], axis=0, keepdims=True)
    out_ref[...] = jnp.where(own_meta[:1] >= 0, top, -1.0)

    @pl.when(jnp.logical_not(is_inner))
    def _():
        sent(0, own)
        for index in (1, 2):
            sent(index, own, (1,), False)

    @pl.when(is_inner)
    def _():
        for index in (1, 2, 5, 6, 7):
            sent(index, own)
        sent(4, own, (0,))

    @pl.when(z == 1)
    def _():
        sent(0, own)
        sent(3, own)
        best_sent(0)

    @pl.when(z == 2)
    def _():
        for index in (0, 1, 2, 3, 5, 6, 7):
            best_sent(index)

        @pl.when(bank == 1)
        def _():
            best_sent(4)
            best_sent(8)


def paired_on_device(embeddings, cluster_of, dest_list):
    rows, width = embeddings.shape
    dma = pltpu.SemaphoreType.DMA
    vmem = pl.BlockSpec(memory_space=pltpu.VMEM)
    result = pl.pallas_call(
        pair_kernel,
        out_shape=jax.ShapeDtypeStruct((1, rows), jnp.float32),
        in_specs=[pl.BlockSpec(memory_space=pltpu.HBM)] * 3,
        out_specs=vmem,
        scratch_shapes=[
            pltpu.VMEM((rows, width), jnp.bfloat16),
            pltpu.VMEM((1, rows), jnp.int32),
            pltpu.VMEM(dest_list.shape[1:], jnp.int32),
            pltpu.VMEM((10, rows, width), jnp.bfloat16),
            pltpu.VMEM((10, 8, rows), jnp.float32),
            pltpu.VMEM((10, rows, 128), jnp.float32),
            pltpu.VMEM((10, 8, rows), jnp.float32),
            pltpu.VMEM((4, 8, rows), jnp.float32),
            pltpu.VMEM((8, rows), jnp.float32),
            dma((3,)), pltpu.SemaphoreType.REGULAR, dma((8, 2)), dma((8,)), dma((10, 2)), dma((10,)), dma((9,)), dma((4,)),
        ],
        compiler_params=pltpu.CompilerParams(
            collective_id=0, has_side_effects=True, vmem_limit_bytes=60 * 2**20
        ),
        cost_estimate=pl.CostEstimate(
            flops=16 * 2 * rows * rows * width, bytes_accessed=rows * width * 2, transcendentals=rows
        ),
    )(embeddings, cluster_of.reshape(1, rows), dest_list[0])
    return result.reshape(rows)


def solution(mesh):
    paired = mesh.shape["bank"] == 2 and mesh.shape["grp"] == 8
    return jax.shard_map(
        paired_on_device if paired else routed_on_device,
        mesh=mesh,
        in_specs=(
            P(("dom", "bank", "grp"), None),
            P(("dom", "bank", "grp")),
            P(("dom", "bank", "grp"), None, None),
        ),
        out_specs=P(("dom", "bank", "grp")),
        check_vma=False,
    )
```

```python
import functools
import jax
import jax.numpy as jnp
from jax import lax
from jax.experimental import pallas as pl
from jax.experimental.pallas import tpu as pltpu
from jax.sharding import PartitionSpec as P

small_eps = 1e-06
MESH = pl.DeviceIdType.MESH


def masked_scores(query_rows, query_cluster, other_rows, other_cluster):
    scores = lax.dot_general(
        query_rows, other_rows, (((1,), (1,)), ((), ())), preferred_element_type=jnp.float32
    )
    matching = query_cluster[:, None] == other_cluster[None, :]
    return (scores, matching)


def routed_on_device(embeddings, cluster_of, dest_list):
    rows_dev = embeddings.shape[0]
    width = embeddings.shape[1]
    devices_part = dest_list.shape[1]
    capacity = dest_list.shape[2]
    source = lax.axis_index(("bank", "grp"))
    widened = embeddings.astype(jnp.float32)
    unit_rows = (
        widened * lax.rsqrt(jnp.sum(widened * widened, axis=1, keepdims=True) + small_eps)
    ).astype(jnp.bfloat16)
    slot_rows = dest_list[0]
    is_live = slot_rows >= 0
    safe_rows = jnp.where(is_live, slot_rows, 0)
    outgoing = jnp.take(unit_rows, safe_rows.reshape(-1), axis=0).reshape(
        devices_part, capacity, width
    )
    out_cluster = jnp.where(is_live, jnp.take(cluster_of, safe_rows), -1)
    out_crawl = jnp.where(is_live, source * rows_dev + safe_rows, -1)
    arrived, in_cluster, in_crawl = (
        lax.all_to_all(outgoing, ("bank", "grp"), split_axis=0, concat_axis=0, tiled=True),
        lax.all_to_all(out_cluster, ("bank", "grp"), split_axis=0, concat_axis=0, tiled=True),
        lax.all_to_all(out_crawl, ("bank", "grp"), split_axis=0, concat_axis=0, tiled=True),
    )
    flat_cluster = in_cluster.reshape(-1)
    flat_crawl = in_crawl.reshape(-1)
    present = flat_cluster >= 0
    position = jnp.cumsum(present.astype(jnp.int32)) - 1
    chosen = (position[None, :] == jnp.arange(rows_dev, dtype=jnp.int32)[:, None]) & present[
        None, :
    ]
    key_rows = jnp.dot(
        chosen.astype(jnp.bfloat16), arrived.reshape(-1, width), preferred_element_type=jnp.float32
    ).astype(jnp.bfloat16)
    key_cluster = jnp.sum(jnp.where(chosen, flat_cluster[None, :], 0), axis=1)
    key_crawl = jnp.sum(jnp.where(chosen, flat_crawl[None, :], 0), axis=1)
    floor_value = jnp.full((rows_dev,), -1.0, jnp.float32)
    scores, matching = masked_scores(
        key_rows,
        key_cluster,
        lax.all_gather(key_rows, "grp", axis=0, tiled=True),
        lax.all_gather(key_cluster, "grp", axis=0, tiled=True),
    )
    earlier = matching & (
        lax.all_gather(key_crawl, "grp", axis=0, tiled=True)[None, :] < key_crawl[:, None]
    )
    best_sim = jnp.maximum(floor_value, jnp.max(jnp.where(earlier, scores, -1.0), axis=1))
    slot_best = jnp.where(
        present, jnp.take(best_sim, jnp.clip(position, 0, rows_dev - 1)), -1.0
    ).reshape(devices_part, capacity)
    returned_best = lax.all_to_all(
        slot_best, ("bank", "grp"), split_axis=0, concat_axis=0, tiled=True
    )
    result = (
        jnp.full((rows_dev,), -1.0, jnp.float32)
        .at[safe_rows.reshape(-1)]
        .max(jnp.where(is_live, returned_best, -1.0).reshape(-1))
    )
    return result


LOW = 8


def pair_kernel(
    emb_hbm, cluster_hbm, dest_hbm, out_ref,
    emb_ref, cluster_ref, dest_ref, blocks, meta, columns, best, returned, own_meta,
    load_sem, ready_sem, block_send, meta_send, block_recv, meta_recv, best_send, best_recv,
):
    loads = [
        pltpu.make_async_copy(source, target, load_sem.at[i])
        for i, (source, target) in enumerate(
            ((emb_hbm, emb_ref), (cluster_hbm, cluster_ref), (dest_hbm, dest_ref))
        )
    ]
    for load in loads:
        load.start()
    rows = emb_ref.shape[0]
    half = rows // 2
    n_dest = dest_ref.shape[0]
    bank = lax.axis_index("bank")
    grp = lax.axis_index("grp")
    z = grp // 2
    x = grp % 2
    high = z // 2
    inner_z = 1 + high
    is_inner = z == inner_z
    mine = 2 * x + bank
    outer_add = jnp.where(is_inner, 0, 4)
    own = mine + outer_add

    barrier = pltpu.get_barrier_semaphore()
    x_grp = z * 2 + (1 - x)
    partner = (1 - bank, grp)
    beside = (bank, x_grp)

    def greet(to_bank, to_grp, sem=barrier):
        pl.semaphore_signal(
            sem, inc=1, device_id={"bank": to_bank, "grp": to_grp}, device_id_type=MESH
        )

    greet(*beside)

    @pl.when(z == 0)
    def _():
        greet(bank, grp + 2)

    @pl.when((z == 0) & (bank == 1))
    def _():
        greet(bank, grp + 4)

    @pl.when(z == 1)
    def _():
        greet(*partner)
        greet(bank, grp - 2)

    @pl.when((z == 1) & (bank == 1))
    def _():
        greet(bank, grp + 2)

    @pl.when(z == 2)
    def _():
        greet(*partner)
        greet(1 - bank, x_grp)
        greet(bank, grp - 2)
        for b in range(2):
            for other_x in range(2):
                greet(b, 6 + other_x)

    loads[0].wait()
    wide = emb_ref[...].astype(jnp.float32)
    scale = lax.rsqrt(jnp.sum(wide * wide, axis=1, keepdims=True) + small_eps)
    blocks[own] = (wide * scale).astype(jnp.bfloat16)

    @pl.when(z == 0)
    def _():
        pl.semaphore_wait(barrier, 2)

    @pl.when(z == 1)
    def _():
        pl.semaphore_wait(barrier, 4)

    @pl.when((z == 2) & (bank == 0))
    def _():
        pl.semaphore_wait(barrier, 3)

    @pl.when((z == 2) & (bank == 1))
    def _():
        pl.semaphore_wait(barrier, 5)

    @pl.when(z == 3)
    def _():
        pl.semaphore_wait(barrier, 5)
        for b in range(2):
            for other_x in range(2):
                greet(b, 4 + other_x, ready_sem)

    def block_copy(index, slot, to_slot, part, to_bank, to_grp):
        span = pl.ds(part * half, half)
        return pltpu.make_async_remote_copy(
            src_ref=blocks.at[slot, span], dst_ref=blocks.at[to_slot, span],
            send_sem=block_send.at[index, part], recv_sem=block_recv.at[to_slot, part],
            device_id={"bank": to_bank, "grp": to_grp}, device_id_type=MESH,
        )

    def meta_copy(index, slot, to_slot, to_bank, to_grp):
        return pltpu.make_async_remote_copy(
            src_ref=meta.at[slot], dst_ref=meta.at[to_slot],
            send_sem=meta_send.at[index], recv_sem=meta_recv.at[to_slot],
            device_id={"bank": to_bank, "grp": to_grp}, device_id_type=MESH,
        )

    def sent(index, slot, parts=(0, 1), with_meta=True):
        if with_meta:
            meta_copy(index, slot, slot, 1 - bank, grp).wait_send()
        for part in parts:
            block_copy(index, slot, slot, part, 1 - bank, grp).wait_send()

    def arrive_meta(slot):
        meta_copy(0, slot, slot, 1 - bank, grp).wait_recv()

    def arrive(slot, part):
        block_copy(0, slot, slot, part, 1 - bank, grp).wait_recv()

    def arrive_all(slot):
        arrive_meta(slot)
        arrive(slot, 0)
        arrive(slot, 1)

    @pl.when(jnp.logical_not(is_inner))
    def _():
        for part in range(2):
            block_copy(0, own, own, part, bank, inner_z * 2 + x).start()
        block_copy(1, own, own, 1, *beside).start()

    @pl.when(z == 1)
    def _():
        for part in range(2):
            block_copy(0, own, LOW, part, bank, grp + 2).start()

    @pl.when(is_inner)
    def _():
        for part in range(2):
            block_copy(1, own, own, part, *beside).start()
        for part in range(2):
            block_copy(2, own, own, part, *partner).start()

    loads[1].wait()
    loads[2].wait()
    row_id = lax.broadcasted_iota(jnp.int32, (dest_ref.shape[1], rows), 1)
    dest_columns = jnp.transpose(dest_ref[...].astype(jnp.float32)).astype(jnp.int32)
    slab_wide = jnp.full(row_id.shape, -1, jnp.int32)
    for d in range(n_dest):
        named = dest_columns[:, d : d + 1] == row_id
        slab_wide = jnp.maximum(slab_wide, jnp.where(named, d // (n_dest // 2), -1))
    slab = jnp.max(slab_wide, axis=0, keepdims=True)
    key = jnp.where(slab >= 0, cluster_ref[...] * 2 + slab, -1).astype(jnp.float32)
    own_meta[...] = jnp.broadcast_to(key, own_meta.shape)
    meta[own] = jnp.broadcast_to(key, own_meta.shape)
    best[...] = jnp.full(best.shape, -1.0, jnp.float32)

    @pl.when(jnp.logical_not(is_inner))
    def _():
        meta_copy(0, own, own, bank, inner_z * 2 + x).start()

    @pl.when(z == 1)
    def _():
        meta_copy(0, own, LOW, bank, grp + 2).start()

    @pl.when(is_inner)
    def _():
        meta_copy(1, own, own, *beside).start()
        meta_copy(2, own, own, *partner).start()

    def column(slot):
        wide_key = jnp.broadcast_to(meta[slot][:1], (128, rows))
        columns[slot] = jnp.transpose(wide_key)

    def slot_of(rel, outer):
        sx = (x + rel // 2) % 2
        sb = (bank + rel % 2) % 2
        slot = 2 * sx + sb + 4 * outer
        sz = inner_z if outer == 0 else 3 * high
        return slot, sb * 8 + sz * 2 + sx

    def scores_into(k_slot, q_slot, diagonal, k_rows=slice(None), q_rows=slice(None)):
        s = lax.dot_general(
            blocks[k_slot, k_rows], blocks[q_slot, q_rows], (((1,), (1,)), ((), ())),
            preferred_element_type=jnp.float32,
        )
        k_key = columns[k_slot, k_rows]
        q_key = meta[q_slot][:1]
        first = q_rows.start or 0
        for h in range(s.shape[1] // 128):
            from_s = slice(h * 128, (h + 1) * 128)
            part = slice(first + h * 128, first + (h + 1) * 128)
            allowed = k_key == q_key[:, part]
            if diagonal:
                k_id = lax.broadcasted_iota(jnp.int32, (rows, 128), 0)
                q_id = lax.broadcasted_iota(jnp.int32, (rows, 128), 1) + h * 128
                allowed = allowed & (k_id < q_id)
            kept = jnp.where(allowed, s[:, from_s], -1.0)
            top = jnp.max(kept.reshape(s.shape[0] // 8, 8, 128), axis=0)
            best[q_slot, :, part] = jnp.maximum(best[q_slot, :, part], top)

    def earlier(k, q):
        @pl.when(k[1] < q[1])
        def _():
            scores_into(k[0], q[0], False)

    def low_pair(which, rel, outer, part=None):
        low = LOW + which
        slot, shard = slot_of(rel, outer)
        low_shard = bank * 8 + (1 - which) * 2 + x
        if part is None:
            low_rows = slice(None)
        else:
            low_rows = slice(part * half, (part + 1) * half)

        @pl.when(low_shard < shard)
        def _():
            scores_into(low, slot, False, low_rows, slice(None))

        @pl.when(low_shard > shard)
        def _():
            scores_into(slot, low, False, slice(None), low_rows)

    @pl.when(is_inner)
    def _():
        in0, in1, in2, in3 = (slot_of(r, 0) for r in range(4))
        out0, out1, out2, out3 = (slot_of(r, 1) for r in range(4))
        column(in0[0])
        scores_into(in0[0], in0[0], True)
        arrive_all(in1[0])
        column(in1[0])
        earlier(in1, in0)

        arrive_meta(out0[0])

        @pl.when(z == 1)
        def _():
            meta_copy(3, out0[0], LOW + 1, bank, grp + 2).start()

        meta_copy(4, out0[0], out0[0], *beside).start()
        meta_copy(5, out0[0], out0[0], *partner).start()
        arrive_meta(in2[0])
        meta_copy(6, in2[0], in2[0], *partner).start()
        column(out0[0])
        column(in2[0])
        for part in range(2):
            arrive(out0[0], part)

            @pl.when(z == 1)
            def _():
                block_copy(3, out0[0], LOW + 1, part, bank, grp + 2).start()

            if part == 0:
                block_copy(4, out0[0], out0[0], part, *beside).start()
            block_copy(5, out0[0], out0[0], part, *partner).start()
            arrive(in2[0], part)
            block_copy(6, in2[0], in2[0], part, *partner).start()
        arrive_meta(out2[0])
        meta_copy(7, out2[0], out2[0], *partner).start()
        column(out2[0])
        scores_into(out0[0], out0[0], True)
        for k, q in ((out0, in0), (in0, out0), (in1, out0), (in2, in0), (in2, out0)):
            earlier(k, q)
        for k in (out1, in3):
            arrive_all(k[0])
            column(k[0])
            earlier(k, in0)
            earlier(k, out0)

        @pl.when(z == 2)
        def _():
            arrive_all(LOW)
            column(LOW)

            @pl.loop(0, 4)
            def _(rel):
                low_pair(0, rel, 0)


        for part in range(2):
            arrive(out2[0], part)
            block_copy(7, out2[0], out2[0], part, *partner).start()

        @pl.when(z == 2)
        def _():
            @pl.loop(0, 2)
            def _(rel):
                low_pair(0, rel, 1)

            arrive_meta(LOW + 1)
            column(LOW + 1)

        @pl.when(z == 2)
        def _():
            for part in range(2):
                arrive(LOW + 1, part)

            @pl.loop(0, 4)
            def _(rel):
                low_pair(1, rel, 0)

            @pl.loop(0, 2)
            def _(rel):
                low_pair(1, rel, 1)

        for rel, k in ((2, out2), (3, out3)):
            if k is out3:
                arrive_all(k[0])
                column(k[0])
            earlier(k, in0)
            earlier(k, out0)

            @pl.when(z == 2)
            def _():
                low_pair(0, rel, 1)
                low_pair(1, rel, 1)

    @pl.when(jnp.logical_not(is_inner))
    def _():
        other = 2 * (1 - x) + bank + 4
        arrive(other, 1)
        block_copy(2, other, other, 1, bank, inner_z * 2 + x).start()

    def best_copy(index, slot, to, to_bank, to_grp):
        return pltpu.make_async_remote_copy(
            src_ref=best.at[slot], dst_ref=returned.at[to],
            send_sem=best_send.at[index], recv_sem=best_recv.at[to],
            device_id={"bank": to_bank, "grp": to_grp}, device_id_type=MESH,
        )

    @pl.when(z == 1)
    def _():
        best_copy(0, mine + 4, 0, bank, grp - 2).start()

    @pl.when(z == 2)
    def _():
        pl.semaphore_wait(ready_sem, 4)
        for rel in range(4):
            slot, _ = slot_of(rel, 0)
            to_bank = (bank + rel % 2) % 2
            to_x = (x + rel // 2) % 2
            best_copy(rel, slot + 4, mine, to_bank, 6 + to_x).start()
            if rel:
                best_copy(4 + rel, slot, mine, to_bank, 4 + to_x).start()

        @pl.when(bank == 1)
        def _():
            best_copy(4, LOW, 1, bank, grp - 2).start()
            best_copy(8, LOW + 1, 1, bank, grp - 4).start()

    def take(index):
        best_copy(0, own, index, 1 - bank, grp).wait_recv()
        best[own] = jnp.maximum(best[own], returned[index])

    def best_sent(index):
        best_copy(index, own, 0, 1 - bank, grp).wait_send()

    @pl.when(z == 0)
    def _():
        take(0)

    @pl.when((z < 2) & (bank == 1))
    def _():
        take(1)

    @pl.when(z >= 2)
    def _():
        for index in range(4):

            @pl.when((z == 3) | (mine != index))
            def _():
                take(index)

    top = jnp.max(best[own], axis=0, keepdims=True)
    out_ref[...] = jnp.where(own_meta[:1] >= 0, top, -1.0)

    @pl.when(jnp.logical_not(is_inner))
    def _():
        sent(0, own)
        for index in (1, 2):
            sent(index, own, (1,), False)

    @pl.when(is_inner)
    def _():
        for index in (1, 2, 5, 6, 7):
            sent(index, own)
        sent(4, own, (0,))

    @pl.when(z == 1)
    def _():
        sent(0, own)
        sent(3, own)
        best_sent(0)

    @pl.when(z == 2)
    def _():
        for index in (0, 1, 2, 3, 5, 6, 7):
            best_sent(index)

        @pl.when(bank == 1)
        def _():
            best_sent(4)
            best_sent(8)


def paired_on_device(embeddings, cluster_of, dest_list):
    rows, width = embeddings.shape
    dma = pltpu.SemaphoreType.DMA
    vmem = pl.BlockSpec(memory_space=pltpu.VMEM)
    result = pl.pallas_call(
        pair_kernel,
        out_shape=jax.ShapeDtypeStruct((1, rows), jnp.float32),
        in_specs=[pl.BlockSpec(memory_space=pltpu.HBM)] * 3,
        out_specs=vmem,
        scratch_shapes=[
            pltpu.VMEM((rows, width), jnp.bfloat16),
            pltpu.VMEM((1, rows), jnp.int32),
            pltpu.VMEM(dest_list.shape[1:], jnp.int32),
            pltpu.VMEM((10, rows, width), jnp.bfloat16),
            pltpu.VMEM((10, 8, rows), jnp.float32),
            pltpu.VMEM((10, rows, 128), jnp.float32),
            pltpu.VMEM((10, 8, rows), jnp.float32),
            pltpu.VMEM((4, 8, rows), jnp.float32),
            pltpu.VMEM((8, rows), jnp.float32),
            dma((3,)), pltpu.SemaphoreType.REGULAR, dma((8, 2)), dma((8,)), dma((10, 2)), dma((10,)), dma((9,)), dma((4,)),
        ],
        compiler_params=pltpu.CompilerParams(
            collective_id=0, has_side_effects=True, vmem_limit_bytes=60 * 2**20
        ),
        cost_estimate=pl.CostEstimate(
            flops=16 * 2 * rows * rows * width, bytes_accessed=rows * width * 2, transcendentals=rows
        ),
    )(embeddings, cluster_of.reshape(1, rows), dest_list[0])
    return result.reshape(rows)


def solution(mesh):
    paired = mesh.shape["bank"] == 2 and mesh.shape["grp"] == 8
    return jax.shard_map(
        paired_on_device if paired else routed_on_device,
        mesh=mesh,
        in_specs=(
            P(("dom", "bank", "grp"), None),
            P(("dom", "bank", "grp")),
            P(("dom", "bank", "grp"), None, None),
        ),
        out_specs=P(("dom", "bank", "grp")),
        check_vma=False,
    )
```
